256 devices in a mesh: rep: 8 (over z_hi, core), mod: 32 (over x, y, z_lo).
Axes of the slice: x: 4, y: 4, z: 8 (z_hi: 4, z_lo: 2; z = z_hi * 2 + z_lo), core: 2. Of those that a mesh axis runs over, the one named last changes fastest.
Arguments:
- table: float32 [64, 2048, 128], P('mod', 'rep'), may hold values from -3 to 3
- accum: float32 [64, 2048], P('mod', 'rep'), may hold values from 0.1 to 10
- bag_rows: int32 [32768, 64, 16], P(('rep', 'mod')), may hold values from 0 to 2047
- pooled_grad: bfloat16 [32768, 64, 128], P(('rep', 'mod')), may hold values from -0.59765625 to 0.59765625
Outputs:
- pooled: bfloat16 [32768, 64, 128], P(('rep', 'mod'))
- new_table: float32 [64, 2048, 128], P('mod')
- new_accum: float32 [64, 2048], P('mod')
The draws below stay inside these ranges and needn't reach their ends.
All inputs are finite; a program needn't handle non-finite values.
Results may differ from the reference program's by a relative error of at most 0.0055.
Values may be sent and summed in bfloat16 or wider, within the bound.
A program may use at most 64 MiB of HBM per device.

```python
import math
import jax
import jax.numpy as jnp
import numpy as np
from jax import lax

E = 128
POOL = 16
ROWS_T = 2048
TABLES = 64
BATCH = 32768


def place_ends(array, stream_key, low, high):
    shape = array.shape
    index_at = [jax.random.randint(jax.random.fold_in(stream_key, axis), (), 0, shape[axis]) for axis in range(len(shape))]
    array = array.at[tuple(index_at)].set(low)
    longest = shape.index(max(shape))
    index_at[longest] = (index_at[longest] + 1) % shape[longest]
    return array.at[tuple(index_at)].set(high)


def shard_levels(stream_key, extent, cuts, least, top_value):
    level = 1.0
    for dim, blocks in cuts:
        heights = jax.random.uniform(jax.random.fold_in(jax.random.fold_in(stream_key, 6), dim), (blocks,), jnp.float32, least / len(cuts), top_value / len(cuts))
        level = level * jnp.repeat(jnp.exp(heights), extent[dim] // blocks).reshape((-1,) + (1,) * (len(extent) - 1 - dim))
    return level


def rank_bounds(number_of, slope):
    portions = [(1 << 20) // math.isqrt(rank ** slope) + 1 for rank in range(1, number_of + 1)]
    deviation = 1 + sum(portions) // (1 << 30)
    return np.cumsum(np.array([max(1, weight // deviation) for weight in portions]))


def ranked_ids(key, dims, number_of, skew):
    table = rank_bounds(number_of, skew)
    ticket = jax.random.randint(jax.random.fold_in(key, 1), dims, 0, int(table[number_of - 1]))
    rank = jnp.searchsorted(jnp.asarray(table, jnp.int32), ticket, side="right")
    return jax.random.permutation(jax.random.fold_in(key, 2), number_of)[rank].astype(jnp.int32)


def normal_values(rng, extent, width, most, shards=(), held_as=jnp.bfloat16):
    values = width * jax.random.normal(rng, extent, jnp.float32)
    if shards:
        values = values * shard_levels(rng, extent, shards, -0.22, 0.18)
    return jnp.clip(values, -most, most).astype(held_as)


def setup_inputs(seed: int = 0) -> dict:
    key_of = jax.random.split(jax.random.key(seed), 5)
    return {
        "table": normal_values(key_of[0], (TABLES, ROWS_T, E), 0.5, 3.0, ((0, 32), (1, 8)), jnp.float32),
        "accum": jnp.clip(jnp.exp(math.log(10.0) - 4.6051702 * jax.random.uniform(key_of[1], (TABLES, ROWS_T), jnp.float32) ** shard_levels(key_of[1], (TABLES, ROWS_T), ((0, 32), (1, 8)), -0.2, 0.2)), 0.1, 10.0),
        "bag_rows": place_ends(ranked_ids(key_of[2], (BATCH, TABLES, POOL), ROWS_T, 2), jax.random.fold_in(key_of[2], 3), 0, ROWS_T - 1).astype(jnp.int32),
        "pooled_grad": normal_values(key_of[3], (BATCH, TABLES, E), 0.1, 0.59765625, ((0, 256),)),
    }


def reference(table, accum, bag_rows, pooled_grad):
    lookup = table.astype(jnp.bfloat16)

    def one_table(index):
        rows = lookup[index]
        ids = bag_rows[:, index, :]
        picked = jnp.take(rows, ids, axis=0).astype(jnp.float32)
        pooled_one = lax.optimization_barrier(jnp.sum(picked, axis=1)).astype(jnp.bfloat16)
        cotan = pooled_grad[:, index, :].astype(jnp.float32)
        spread = jnp.broadcast_to(cotan[:, None, :], (BATCH, POOL, E)).reshape(BATCH * POOL, E)
        grad = jax.ops.segment_sum(spread, ids.reshape(BATCH * POOL), num_segments=ROWS_T)
        return (pooled_one, grad)
    pooled_all, row_grad = lax.map(one_table, jnp.arange(TABLES, dtype=jnp.int32))
    pooled = jnp.transpose(pooled_all, (1, 0, 2))
    new_accum = accum + lax.optimization_barrier(jnp.mean(row_grad * row_grad, axis=-1))
    new_table = table - 0.1 * row_grad / jnp.sqrt(new_accum)[:, :, None]
    return (pooled, new_table, new_accum)
```

```python
import functools

import jax
import jax.numpy as jnp
from jax import lax
from jax.experimental import pallas as pl
from jax.experimental.pallas import tpu as pltpu
from jax.sharding import PartitionSpec as P

BF16, F32 = jnp.bfloat16, jnp.float32
SUB = 8
HIGH = 8


def pool_kernel(blocks, unroll, ids_ref, cot_ref, table_ref, pooled_ref, grad_ref, high_key, low_key, counts, total):
    rows = table_ref.shape[1]
    low = rows // HIGH
    pair_rows = 2 * SUB
    step = pl.program_id(0)
    ids = ids_ref[...]
    lane = lax.broadcasted_iota(jnp.int32, ids.shape, 1)
    high_key[...] = ((ids // low) * pair_rows + lane // (256 // pair_rows)).astype(F32)
    low_key[...] = (ids % low).astype(F32)
    iota = lax.broadcasted_iota(jnp.int32, (pair_rows, 256), 0).astype(F32)
    one, zero = jnp.ones((pair_rows, 256), BF16), jnp.zeros((pair_rows, 256), BF16)

    def count_block(b, _):
        high_row = jnp.broadcast_to(high_key[pl.ds(b, 1), :], (pair_rows, 256)).astype(BF16)
        low_row = jnp.broadcast_to(low_key[pl.ds(b, 1), :], (pair_rows, 256)).astype(BF16)
        high_hot = jnp.concatenate(
            [jnp.where(high_row == (iota + pair_rows * i).astype(BF16), one, zero) for i in range(HIGH)], 0
        )
        low_hot = jnp.concatenate(
            [jnp.where(low_row == (iota + pair_rows * i).astype(BF16), one, zero) for i in range(low // pair_rows)], 0
        )
        out = lax.dot_general(high_hot, low_hot, (((1,), (1,)), ((), ())), preferred_element_type=F32).astype(BF16)
        at = pl.multiple_of(b * pair_rows, pair_rows)
        for i in range(HIGH):
            counts[pl.ds(at, pair_rows), i * low : (i + 1) * low] = out[i * pair_rows : (i + 1) * pair_rows]
        return 0

    lax.fori_loop(0, blocks, count_block, 0, unroll=unroll)
    both = jnp.concatenate([table_ref[0], table_ref[1]], 1)
    sums = jnp.dot(counts[...], both, preferred_element_type=F32)
    parity = lax.broadcasted_iota(jnp.int32, (blocks * pair_rows, 128), 0) % 2
    pooled_ref[...] = jnp.where(parity == 0, sums[:, :128], sums[:, 128:]).astype(BF16)
    cot = cot_ref[...]
    second = cot * parity.astype(F32).astype(BF16)
    split = jnp.concatenate([cot - second, second], 1)
    grad = lax.dot_general(split, counts[...], (((0,), (0,)), ((), ())), preferred_element_type=F32)

    @pl.when(step == 0)
    def _():
        total[...] = grad

    @pl.when(step > 0)
    def _():
        total[...] += grad

    @pl.when(step == pl.num_programs(0) - 1)
    def _():
        grad_ref[0] = total[:128].T.astype(BF16)
        grad_ref[1] = total[128:].T.astype(BF16)


def pool_and_grad(ids, cot, lookup, blocks=64, unroll=16):
    all_blocks, rows = ids.shape[0], lookup.shape[1]
    height = blocks * 2 * SUB
    return pl.pallas_call(
        functools.partial(pool_kernel, blocks, unroll),
        grid=(all_blocks // blocks,),
        out_shape=[
            jax.ShapeDtypeStruct((all_blocks * 2 * SUB, 128), BF16),
            jax.ShapeDtypeStruct((2, rows, 128), BF16),
        ],
        in_specs=[
            pl.BlockSpec((blocks, 256), lambda i: (i, 0)),
            pl.BlockSpec((height, 128), lambda i: (i, 0)),
            pl.BlockSpec((2, rows, 128), lambda i: (0, 0, 0)),
        ],
        out_specs=[
            pl.BlockSpec((height, 128), lambda i: (i, 0)),
            pl.BlockSpec((2, rows, 128), lambda i: (0, 0, 0)),
        ],
        scratch_shapes=[
            pltpu.VMEM((blocks, 256), F32),
            pltpu.VMEM((blocks, 256), F32),
            pltpu.VMEM((height, rows), BF16),
            pltpu.VMEM((256, rows), F32),
        ],
        compiler_params=pltpu.CompilerParams(vmem_limit_bytes=48 << 20),
        name="pool_and_grad",
    )(ids, cot, lookup)


def adagrad(weights, sums, grad):
    new_sums = sums + jnp.mean(grad * grad, axis=-1)
    new_weights = weights - 0.1 * grad / jnp.sqrt(new_sums)[:, :, None]
    return (new_weights, new_sums)


def local(table, accum, bag_rows, pooled_grad):
    samples, tables, pool_len = bag_rows.shape
    pairs = tables // 2
    ids = bag_rows.astype(jnp.int16).reshape(samples // SUB, SUB, pairs, 2, pool_len)
    ids = ids.transpose(2, 0, 1, 3, 4).reshape(pairs, samples // SUB, SUB * 2 * pool_len)
    group_ids = lax.all_to_all(ids, "mod", split_axis=0, concat_axis=0, tiled=True)
    cot = pooled_grad.reshape(samples, pairs, 2, 128).transpose(1, 0, 2, 3).reshape(pairs, samples * 2, 128)
    group_cot = lax.all_to_all(cot, "mod", split_axis=0, concat_axis=0, tiled=True)
    full_accum = lax.all_gather(accum, "rep", axis=1, tiled=True)
    full_table = lax.all_gather(table, "rep", axis=1, tiled=True)
    pooled_group, row_grad = pool_and_grad(
        group_ids.reshape(-1, 256).astype(jnp.int32), group_cot.reshape(-1, 128), full_table.astype(BF16)
    )
    pooled = lax.all_to_all(pooled_group.reshape(pairs, samples * 2, 128), "mod", split_axis=0, concat_axis=0, tiled=True)
    pooled = pooled.reshape(pairs, samples, 2, 128).transpose(1, 0, 2, 3).reshape(samples, tables, 128)
    total = lax.psum(row_grad, "rep").astype(F32)
    new_table, new_accum = adagrad(full_table, full_accum, total)
    return (pooled, new_table, new_accum)


def solution(mesh):
    in_specs = (
        P("mod", "rep", None),
        P("mod", "rep"),
        P(("rep", "mod"), None, None),
        P(("rep", "mod"), None, None),
    )
    out_specs = (P(("rep", "mod"), None, None), P("mod", None, None), P("mod", None))
    return jax.shard_map(local, mesh=mesh, in_specs=in_specs, out_specs=out_specs, check_vma=False)
```

```python
import functools

import jax
import jax.numpy as jnp
from jax import lax
from jax.experimental import pallas as pl
from jax.experimental.pallas import tpu as pltpu
from jax.sharding import PartitionSpec as P

BF16, F32, I32 = jnp.bfloat16, jnp.float32, jnp.int32
SUB = 8
HIGH = 8
LOW = 256
PEERS = 32
CHUNK = 256
BATCHED = 4
GROUPS = PEERS // BATCHED
LAG = 2
STRIDE = 11
MESH = pl.DeviceIdType.MESH


def away(me, step, sign):
    x, y, z = me // 8, (me // 2) % 4, me % 2
    dx, dy, dz = step // 8, (step // 2) % 4, step % 2
    return ((x + sign * dx + 4) % 4) * 8 + ((y + sign * dy + 4) % 4) * 2 + (z + dz) % 2


def order(i):
    return (i * STRIDE) % PEERS


def step_kernel(
    ids_ref, cot_ref, table_ref, accum_ref, pooled_ref, new_table_ref, new_accum_ref,
    ids_buf, cot_buf, pooled_buf, shards, both, high_key, low_key, counts, split,
    pair_out, pair_in, ring_out, ring_in, own_grad, new_shard, new_sums,
    ids_out, ids_in, cot_out, cot_in, pool_out, pool_in, local_sem,
    tab_out, tab_in, tab_fwd_out, tab_fwd_in, px_out, px_in, rs_out, rs_in,
    new_out, new_in, fwd_out, fwd_in, acc_out, acc_in,
):
    me = lax.axis_index("mod")
    rep = lax.axis_index("rep")
    high, core = rep // 2, rep % 2
    twin = {"rep": high * 2 + 1 - core}

    def ring(step):
        return {"rep": ((high + step + 4) % 4) * 2 + core}

    def remote(src, dst, out_sem, in_sem, device):
        return pltpu.make_async_remote_copy(
            src_ref=src, dst_ref=dst, send_sem=out_sem, recv_sem=in_sem, device_id=device, device_id_type=MESH
        )

    def ids_copy(k):
        return remote(ids_ref.at[away(me, k, 1)], ids_buf.at[k], ids_out.at[k], ids_in.at[k], {"mod": away(me, k, 1)})

    def cot_copy(k):
        return remote(cot_ref.at[:, away(me, k, 1)], cot_buf.at[k], cot_out.at[k], cot_in.at[k], {"mod": away(me, k, 1)})

    def pool_copy(k):
        return remote(pooled_buf.at[k], pooled_ref.at[:, me], pool_out.at[k], pool_in.at[k], {"mod": away(me, k, -1)})

    def pool_arrival(k):
        return remote(
            pooled_buf.at[k], pooled_ref.at[:, away(me, k, 1)], pool_out.at[k], pool_in.at[k], {"mod": away(me, k, -1)}
        )

    def shard_copy(step, device, out_sem, in_sem, offset=0):
        at = ((high + offset + 4) % 4) * 2 + core
        return remote(shards.at[at], shards.at[at], out_sem.at[step], in_sem.at[step], device)

    barrier = pltpu.get_barrier_semaphore()

    @pl.loop(1, PEERS)
    def _(k):
        pl.semaphore_signal(barrier, inc=1, device_id={"mod": away(me, k, 1)}, device_id_type=MESH)

    @pl.loop(0, 8)
    def _(r):
        @pl.when(r != rep)
        def _():
            pl.semaphore_signal(barrier, inc=1, device_id={"rep": r}, device_id_type=MESH)

    own_ids = pltpu.make_async_copy(ids_ref.at[me], ids_buf.at[0], local_sem.at[0])
    own_cot = pltpu.make_async_copy(cot_ref.at[:, me], cot_buf.at[0], local_sem.at[1])
    own_ids.start()
    own_cot.start()
    shards[rep] = table_ref[...].astype(BF16)
    pl.semaphore_wait(barrier, PEERS - 1 + 7)

    @pl.loop(1, PEERS)
    def _(i):
        ids_copy(order(i)).start()

    for step in (1, 3, 2):
        shard_copy(step, ring(step), tab_out, tab_in).start()
    shard_copy(0, twin, tab_fwd_out, tab_fwd_in).start()

    @pl.loop(1, PEERS)
    def _(i):
        cot_copy(order(i)).start()

    own_ids.wait()
    own_cot.wait()

    lane = lax.broadcasted_iota(I32, (16, 256), 1)
    iota = lax.broadcasted_iota(I32, (16, 256), 0).astype(F32)
    one, zero = jnp.ones((16, 256), BF16), jnp.zeros((16, 256), BF16)
    sample3 = lax.broadcasted_iota(I32, (16, SUB, 128), 1)
    lane3 = lax.broadcasted_iota(I32, (16, SUB, 128), 2) // 32

    def count_chunk(i):
        k = order(i)

        @pl.when(i > 0)
        def _():
            ids_copy(k).wait_recv()

        ids = ids_buf[k].astype(I32).astype(F32)
        turned = jnp.concatenate([ids] * 4, 0).T.reshape(16, SUB, 128)
        first = jnp.sum(jnp.where(sample3 == lane3, turned, 0.0), axis=1)
        second = jnp.sum(jnp.where(sample3 == lane3 + 4, turned, 0.0), axis=1)
        flat = jnp.concatenate([first, second], 1).astype(I32)
        high_key[...] = ((flat // LOW) * 16 + lane // 16).astype(F32)
        low_key[...] = (flat % LOW).astype(F32)
        base = pl.multiple_of(i * CHUNK, CHUNK)
        for b in range(16):
            high_row = jnp.broadcast_to(high_key[b : b + 1, :], (16, 256)).astype(BF16)
            low_row = jnp.broadcast_to(low_key[b : b + 1, :], (16, 256)).astype(BF16)
            high_hot = jnp.concatenate(
                [jnp.where(high_row == (iota + 16 * j).astype(BF16), one, zero) for j in range(HIGH)], 0
            )
            low_hot = jnp.concatenate(
                [jnp.where(low_row == (iota + 16 * j).astype(BF16), one, zero) for j in range(LOW // 16)], 0
            )
            out = lax.dot_general(high_hot, low_hot, (((1,), (1,)), ((), ())), preferred_element_type=F32).astype(BF16)
            for j in range(HIGH):
                counts[j, pl.ds(base + b * 16, 16), :] = out[j * 16 : (j + 1) * 16]

    parity = lax.broadcasted_iota(I32, (BATCHED * CHUNK, 128), 0) % 2
    odd = (lax.broadcasted_iota(I32, (128, CHUNK), 1) % 2).astype(F32).astype(BF16)

    def pool_group(g):
        base = pl.multiple_of(g * BATCHED * CHUNK, BATCHED * CHUNK)
        rows = jnp.concatenate([counts[j, pl.ds(base, BATCHED * CHUNK), :] for j in range(HIGH)], 1)
        sums = jnp.dot(rows, both[...], preferred_element_type=F32)
        picked = jnp.where(parity == 0, sums[:, :128], sums[:, 128:]).astype(BF16)
        for b in range(BATCHED):
            pooled_buf[order(g * BATCHED + b)] = picked[b * CHUNK : (b + 1) * CHUNK].reshape(CHUNK // 2, 2, 128)
        for b in range(BATCHED):
            i = g * BATCHED + b

            @pl.when(i > 0)
            def _(i=i):
                pool_copy(order(i)).start()

    def turn_cotangents(g):
        @pl.loop(0, BATCHED)
        def _(b):
            i = g * BATCHED + b
            k = order(i)

            @pl.when(i > 0)
            def _():
                cot_copy(k).wait_recv()

            turned = cot_buf[k].reshape(CHUNK, 128).T
            at = pl.ds(pl.multiple_of(i * CHUNK, CHUNK), CHUNK)
            second = turned * odd
            split[0:128, at] = turned - second
            split[128:256, at] = second

    @pl.loop(0, GROUPS + LAG)
    def _(g):
        @pl.when(g < GROUPS)
        def _():
            @pl.loop(0, BATCHED)
            def _(b):
                count_chunk(g * BATCHED + b)

        @pl.when(g == 0)
        def _():
            for step in (1, 3, 2):
                shard_copy(step, ring(step), tab_out, tab_in, -step).wait_recv()
                shard_copy(step, twin, tab_fwd_out, tab_fwd_in, -step).start()

        @pl.when(g == LAG)
        def _():
            for step in range(4):
                at = ((high - step + 4) % 4) * 2 + 1 - core
                remote(shards.at[at], shards.at[at], tab_fwd_out.at[step], tab_fwd_in.at[step], twin).wait_recv()
            for j in range(HIGH):
                both[j * LOW : (j + 1) * LOW, :] = jnp.concatenate([shards[j, 0], shards[j, 1]], 1)

        @pl.when(g >= LAG)
        def _():
            pool_group(g - LAG)
            turn_cotangents(g - LAG)

    own_pool = pltpu.make_async_copy(pooled_buf.at[0], pooled_ref.at[:, me], local_sem.at[2])
    own_pool.start()

    def grad_block(at):
        return jnp.dot(split[...], counts[at], preferred_element_type=F32)

    def pair_copy(step):
        return remote(pair_out.at[step], pair_in.at[step], px_out.at[step], px_in.at[step], twin)

    def ring_copy(step):
        return remote(ring_out.at[step], ring_in.at[step], rs_out.at[step], rs_in.at[step], ring(step))

    @pl.loop(1, 5)
    def _(n):
        step = n % 4
        pair_out[step] = grad_block(((high + step) % 4) * 2 + 1 - core).astype(BF16)
        pair_copy(step).start()

    @pl.loop(1, 5)
    def _(n):
        step = n % 4
        own = grad_block(((high + step) % 4) * 2 + core)
        pair_copy(step).wait_recv()
        total = own + pair_in[step].astype(F32)

        @pl.when(step > 0)
        def _():
            ring_out[step] = total.astype(BF16)
            ring_copy(step).start()

        @pl.when(step == 0)
        def _():
            own_grad[...] = total

    for step in (1, 2, 3):
        ring_copy(step).wait_recv()
    grad = own_grad[...] + ring_in[1].astype(F32) + ring_in[2].astype(F32) + ring_in[3].astype(F32)
    for t in range(2):
        one_grad = grad[t * 128 : (t + 1) * 128]
        sums = accum_ref[t : t + 1, :] + jnp.mean(one_grad * one_grad, axis=0, keepdims=True)
        new_sums[t : t + 1, :] = sums
        new_shard[t] = table_ref[t] - (0.1 * one_grad / jnp.sqrt(sums)).T

    here = pl.ds(pl.multiple_of(rep * LOW, LOW), LOW)
    own_new = pltpu.make_async_copy(new_shard, new_table_ref.at[:, rep], local_sem.at[3])
    own_sums = pltpu.make_async_copy(new_sums, new_accum_ref.at[:, here], local_sem.at[4])

    def new_copy(step, device):
        return remote(new_shard, new_table_ref.at[:, rep], new_out.at[step], new_in.at[step], device)

    def new_arrival(step, device):
        at = ((high - step + 4) % 4) * 2 + core
        return remote(new_shard, new_table_ref.at[:, at], new_out.at[step], new_in.at[step], device)

    def new_forward(step):
        at = ((high - step + 4) % 4) * 2 + core
        return remote(new_table_ref.at[:, at], new_table_ref.at[:, at], fwd_out.at[step], fwd_in.at[step], twin)

    def sums_copy(r, at):
        where = pl.ds(pl.multiple_of(at * LOW, LOW), LOW)
        return remote(new_sums, new_accum_ref.at[:, where], acc_out.at[r], acc_in.at[r], {"rep": (rep + r) % 8})

    for step in (1, 3, 2):
        new_copy(step, ring(step)).start()
    new_twin = remote(new_shard, new_table_ref.at[:, rep], fwd_out.at[0], fwd_in.at[0], twin)
    new_twin.start()

    @pl.loop(1, 8)
    def _(r):
        sums_copy(r, rep).start()

    own_new.start()
    own_sums.start()
    for step in (1, 3, 2):
        new_arrival(step, ring(step)).wait_recv()
        new_forward(step).start()
    for step in range(4):
        at = ((high - step + 4) % 4) * 2 + 1 - core
        remote(new_table_ref.at[:, at], new_table_ref.at[:, at], fwd_out.at[step], fwd_in.at[step], twin).wait_recv()

    @pl.loop(1, 8)
    def _(r):
        sums_copy(r, (rep - r + 8) % 8).wait_recv()

    @pl.loop(1, PEERS)
    def _(k):
        pool_arrival(k).wait_recv()

    own_pool.wait()
    own_new.wait()
    own_sums.wait()

    @pl.loop(1, PEERS)
    def _(k):
        ids_copy(k).wait_send()
        cot_copy(k).wait_send()
        pool_copy(k).wait_send()

    for step in (1, 2, 3):
        shard_copy(step, ring(step), tab_out, tab_in).wait_send()
        shard_copy(step, twin, tab_fwd_out, tab_fwd_in, -step).wait_send()
        ring_copy(step).wait_send()
        new_copy(step, ring(step)).wait_send()
        new_forward(step).wait_send()
    shard_copy(0, twin, tab_fwd_out, tab_fwd_in).wait_send()
    new_twin.wait_send()
    for step in range(4):
        pair_copy(step).wait_send()

    @pl.loop(1, 8)
    def _(r):
        sums_copy(r, rep).wait_send()


def local(table, accum, bag_rows, pooled_grad):
    samples, tables, pool_len = bag_rows.shape
    pairs = tables // 2
    ids = bag_rows.transpose(1, 2, 0).astype(jnp.int16).reshape(pairs, 2 * pool_len, samples)
    cot = pooled_grad.reshape(samples, pairs, 2, 128)
    rows = PEERS * CHUNK
    dma = pltpu.SemaphoreType.DMA
    pooled, new_table, new_accum = pl.pallas_call(
        step_kernel,
        out_shape=[
            jax.ShapeDtypeStruct((samples, pairs, 2, 128), BF16),
            jax.ShapeDtypeStruct((2, 8, LOW, 128), F32),
            jax.ShapeDtypeStruct((2, 8 * LOW), F32),
        ],
        in_specs=[
            pl.BlockSpec(memory_space=pl.ANY),
            pl.BlockSpec(memory_space=pl.ANY),
            pl.BlockSpec(memory_space=pltpu.VMEM),
            pl.BlockSpec(memory_space=pltpu.VMEM),
        ],
        out_specs=[pl.BlockSpec(memory_space=pl.ANY)] * 3,
        scratch_shapes=[
            pltpu.VMEM((PEERS, 32, 128), jnp.int16),
            pltpu.VMEM((PEERS, CHUNK // 2, 2, 128), BF16),
            pltpu.VMEM((PEERS, CHUNK // 2, 2, 128), BF16),
            pltpu.VMEM((8, 2, LOW, 128), BF16),
            pltpu.VMEM((HIGH * LOW, 256), BF16),
            pltpu.VMEM((16, 256), F32),
            pltpu.VMEM((16, 256), F32),
            pltpu.VMEM((HIGH, rows, LOW), BF16),
            pltpu.VMEM((256, rows), BF16),
            pltpu.VMEM((4, 256, LOW), BF16),
            pltpu.VMEM((4, 256, LOW), BF16),
            pltpu.VMEM((4, 256, LOW), BF16),
            pltpu.VMEM((4, 256, LOW), BF16),
            pltpu.VMEM((256, LOW), F32),
            pltpu.VMEM((2, LOW, 128), F32),
            pltpu.VMEM((2, LOW), F32),
        ]
        + [dma((PEERS,))] * 6
        + [dma((5,))]
        + [dma((4,))] * 12
        + [dma((8,))] * 2,
        compiler_params=pltpu.CompilerParams(collective_id=1, has_side_effects=True, vmem_limit_bytes=58 << 20),
        name="embedding_step",
    )(ids, cot, table, accum)
    return (pooled.reshape(samples, tables, 128), new_table.reshape(2, 8 * LOW, 128), new_accum)


def solution(mesh):
    in_specs = (
        P("mod", "rep", None),
        P("mod", "rep"),
        P(("rep", "mod"), None, None),
        P(("rep", "mod"), None, None),
    )
    out_specs = (P(("rep", "mod"), None, None), P("mod", None, None), P("mod", None))
    return jax.shard_map(local, mesh=mesh, in_specs=in_specs, out_specs=out_specs, check_vma=False)
```

```python
import functools

import jax
import jax.numpy as jnp
from jax import lax
from jax.experimental import pallas as pl
from jax.experimental.pallas import tpu as pltpu
from jax.sharding import PartitionSpec as P

BF16, F32, I32 = jnp.bfloat16, jnp.float32, jnp.int32
SUB = 8
HIGH = 16
LOW = 128
SHARD = 256
PEERS = 32
CHUNK = 256
BATCHED = 4
GROUPS = PEERS // BATCHED
EARLY, MIDDLE, LATE = 4, 6, 8
STRIDE = 11
MESH = pl.DeviceIdType.MESH


def away(me, step, sign):
    x, y, z = me // 8, (me // 2) % 4, me % 2
    dx, dy, dz = step // 8, (step // 2) % 4, step % 2
    return ((x + sign * dx + 4) % 4) * 8 + ((y + sign * dy + 4) % 4) * 2 + (z + dz) % 2


def order(i):
    return (i * STRIDE) % PEERS


def step_kernel(
    wide_ids_ref, cot_ref, table_ref, accum_ref, pooled_ref, new_table_ref, new_accum_ref,
    ids_ref, ids_buf, cot_buf, pooled_buf, shards, both, high_key, low_key, counts, split,
    pair_out, pair_in, far_out, far_in, near_out, near_in, new_shard, new_sums,
    ids_out, ids_in, cot_out, cot_in, pool_out, pool_in, local_sem,
    tab_out, tab_in, tab_twin_out, tab_twin_in, px_out, px_in, far_sem_out, far_sem_in, near_sem_out, near_sem_in,
    new_out, new_in, new_twin_out, new_twin_in, acc_out, acc_in,
):
    me = lax.axis_index("mod")
    rep = lax.axis_index("rep")
    high, core = rep // 2, rep % 2
    twin = {"rep": high * 2 + 1 - core}

    x, y, z = me // 8, (me // 2) % 4, me % 2
    xs = [((x + d) % 4) * 8 for d in range(4)]
    ys = [((y + d) % 4) * 2 for d in range(4)]
    zs = [(z + d) % 2 for d in range(2)]

    def peer(k, sign):
        if not isinstance(k, int):
            return away(me, k, sign)
        return xs[(sign * (k // 8)) % 4] + ys[(sign * (k // 2)) % 4] + zs[k % 2]

    def ring(step):
        return {"rep": ((high + step + 4) % 4) * 2 + core}

    def remote(src, dst, out_sem, in_sem, device):
        return pltpu.make_async_remote_copy(
            src_ref=src, dst_ref=dst, send_sem=out_sem, recv_sem=in_sem, device_id=device, device_id_type=MESH
        )

    def ids_copy(k):
        return remote(ids_ref.at[peer(k, 1)], ids_buf.at[k], ids_out.at[k], ids_in.at[k], {"mod": peer(k, 1)})

    def cot_copy(k):
        return remote(cot_ref.at[:, peer(k, 1)], cot_buf.at[k], cot_out.at[k], cot_in.at[k], {"mod": peer(k, 1)})

    def pool_copy(k):
        return remote(pooled_buf.at[k], pooled_ref.at[:, me], pool_out.at[k], pool_in.at[k], {"mod": peer(k, -1)})

    def pool_arrival(k):
        return remote(
            pooled_buf.at[k], pooled_ref.at[:, peer(k, 1)], pool_out.at[k], pool_in.at[k], {"mod": peer(k, -1)}
        )

    def slot(offset, other=0):
        return ((high + offset + 4) % 4) * 2 + (core + other - 2 * core * other)

    def ring_near(ref, n, out_sem, in_sem, arrival=False):
        table, side = (n, 1) if n < 2 else (3 - n, -1)
        at = ref.at[table, slot(-side if arrival else 0)]
        return remote(at, at, out_sem.at[n], in_sem.at[n], ring(side))

    def ring_far(ref, n, out_sem, in_sem, arrival=False):
        table, side = (0, 1) if n == 0 else (1, -1)
        at = ref.at[table, slot(2 if arrival else -side)]
        return remote(at, at, out_sem.at[4 + n], in_sem.at[4 + n], ring(side))

    def twin_copy(ref, offset, table, out_sem, in_sem, arrival=False):
        at = ref.at[table, slot(offset, 1 if arrival else 0)]
        n = (offset + 4) % 4 * 2 + table
        return remote(at, at, out_sem.at[n], in_sem.at[n], twin)

    def spread_own(ref, out_sem, in_sem, twin_out, twin_in):
        for n in (0, 2, 1, 3):
            ring_near(ref, n, out_sem, in_sem).start()
        for table in range(2):
            twin_copy(ref, 0, table, twin_out, twin_in).start()

    def spread_near(ref, out_sem, in_sem, twin_out, twin_in):
        for n in range(2):
            ring_near(ref, 2 * n, out_sem, in_sem, True).wait_recv()
            ring_far(ref, n, out_sem, in_sem).start()
            twin_copy(ref, -1 if n == 0 else 1, n, twin_out, twin_in).start()

    def spread_rest(ref, out_sem, in_sem, twin_out, twin_in):
        for n in range(2):
            ring_near(ref, 2 * n + 1, out_sem, in_sem, True).wait_recv()
            twin_copy(ref, -1 if n == 0 else 1, 1 - n, twin_out, twin_in).start()
        for n in range(2):
            ring_far(ref, n, out_sem, in_sem, True).wait_recv()
            twin_copy(ref, 2, n, twin_out, twin_in).start()

    def spread_end(ref, twin_out, twin_in):
        for offset in range(4):
            for table in range(2):
                twin_copy(ref, offset, table, twin_out, twin_in, True).wait_recv()

    def spread_sent(ref, out_sem, in_sem, twin_out, twin_in):
        for n in range(4):
            ring_near(ref, n, out_sem, in_sem).wait_send()
        for n in range(2):
            ring_far(ref, n, out_sem, in_sem).wait_send()
        for offset in range(4):
            for table in range(2):
                twin_copy(ref, offset, table, twin_out, twin_in).wait_send()

    barrier = pltpu.get_barrier_semaphore()

    for k in range(1, PEERS):
        pl.semaphore_signal(barrier, inc=1, device_id={"mod": peer(k, 1)}, device_id_type=MESH)
    for r in range(1, 8):
        pl.semaphore_signal(barrier, inc=1, device_id={"rep": (rep + r) % 8}, device_id_type=MESH)

    own_cot = pltpu.make_async_copy(cot_ref.at[:, me], cot_buf.at[0], local_sem.at[1])
    own_cot.start()

    @pl.loop(0, PEERS)
    def _(k):
        ids_ref[k] = wide_ids_ref[k].astype(jnp.int16)

    ids_buf[0] = ids_ref[me]
    shards[0, rep] = table_ref[0].astype(BF16)
    shards[1, rep] = table_ref[1].astype(BF16)
    pl.semaphore_wait(barrier, PEERS - 1 + 7)

    for i in range(1, PEERS):
        ids_copy(order(i)).start()

    spread_own(shards, tab_out, tab_in, tab_twin_out, tab_twin_in)

    for i in range(1, PEERS):
        cot_copy(order(i)).start()

    own_cot.wait()

    lane = lax.broadcasted_iota(I32, (16, 256), 1)
    iota = lax.broadcasted_iota(I32, (16, 256), 0).astype(F32)
    one, zero = jnp.ones((16, 256), BF16), jnp.zeros((16, 256), BF16)
    sample3 = lax.broadcasted_iota(I32, (16, SUB, 128), 1)
    lane3 = lax.broadcasted_iota(I32, (16, SUB, 128), 2) // 32

    def count_chunks(first):
        for c in range(2):
            i = first + c
            k = order(i)

            if c > 0:
                ids_copy(k).wait_recv()
            else:

                @pl.when(i > 0)
                def _(k=k):
                    ids_copy(k).wait_recv()

        for c in range(2):
            ids = ids_buf[order(first + c)].astype(I32).astype(F32)
            turned = jnp.concatenate([ids] * 4, 0).T.reshape(16, SUB, 128)
            upper = jnp.sum(jnp.where(sample3 == lane3, turned, 0.0), axis=1)
            lower = jnp.sum(jnp.where(sample3 == lane3 + 4, turned, 0.0), axis=1)
            flat = jnp.concatenate([upper, lower], 1).astype(I32)
            high_key[c * 16 : (c + 1) * 16] = ((flat // LOW) * 16 + lane // 16).astype(F32)
            low_key[c * 16 : (c + 1) * 16] = (flat % LOW).astype(F32)
        base = pl.multiple_of(first * CHUNK, 2 * CHUNK)
        for b in range(32):
            high_row = jnp.broadcast_to(high_key[b : b + 1, :], (16, 256)).astype(BF16)
            low_row = jnp.broadcast_to(low_key[b : b + 1, :], (16, 256)).astype(BF16)
            high_hot = jnp.concatenate(
                [jnp.where(high_row == (iota + 16 * j).astype(BF16), one, zero) for j in range(HIGH)], 0
            )
            low_hot = jnp.concatenate(
                [jnp.where(low_row == (iota + 16 * j).astype(BF16), one, zero) for j in range(LOW // 16)], 0
            )
            out = lax.dot_general(high_hot, low_hot, (((1,), (1,)), ((), ())), preferred_element_type=F32).astype(BF16)
            for j in range(HIGH):
                counts[j, pl.ds(base + b * 16, 16), :] = out[j * 16 : (j + 1) * 16]

    parity = lax.broadcasted_iota(I32, (BATCHED * CHUNK, 128), 0) % 2
    odd = (lax.broadcasted_iota(I32, (128, CHUNK), 1) % 2).astype(F32).astype(BF16)

    def pool_group(g):
        base = pl.multiple_of(g * BATCHED * CHUNK, BATCHED * CHUNK)
        rows = jnp.concatenate([counts[j, pl.ds(base, BATCHED * CHUNK), :] for j in range(HIGH)], 1)
        sums = jnp.dot(rows, both[...], preferred_element_type=F32)
        picked = jnp.where(parity == 0, sums[:, :128], sums[:, 128:]).astype(BF16)
        for b in range(BATCHED):
            pooled_buf[order(g * BATCHED + b)] = picked[b * CHUNK : (b + 1) * CHUNK].reshape(CHUNK // 2, 2, 128)
        for b in range(BATCHED):
            i = g * BATCHED + b

            @pl.when(i > 0)
            def _(i=i):
                pool_copy(order(i)).start()

    def pool_groups(start, end):
        if end > start:

            @pl.loop(start, end)
            def _(g):
                pool_group(g)

    def turn_cotangents(g):
        @pl.loop(0, BATCHED)
        def _(b):
            i = g * BATCHED + b
            k = order(i)

            @pl.when(i > 0)
            def _():
                cot_copy(k).wait_recv()

            turned = cot_buf[k].reshape(CHUNK, 128).T
            at = pl.ds(pl.multiple_of(i * CHUNK, CHUNK), CHUNK)
            second = turned * odd
            split[0:128, at] = turned - second
            split[128:256, at] = second

    @pl.loop(0, GROUPS)
    def _(g):
        @pl.loop(0, BATCHED // 2)
        def _(b):
            count_chunks(g * BATCHED + 2 * b)

        @pl.when(g == 3)
        def _():
            spread_near(shards, tab_out, tab_in, tab_twin_out, tab_twin_in)

        @pl.when(g == 6)
        def _():
            spread_rest(shards, tab_out, tab_in, tab_twin_out, tab_twin_in)

    spread_end(shards, tab_twin_out, tab_twin_in)
    for j in range(8):
        both[j * SHARD : (j + 1) * SHARD, :] = jnp.concatenate([shards[0, j], shards[1, j]], 1)

    @pl.loop(0, EARLY)
    def _(g):
        pool_group(g)

    own_pool = pltpu.make_async_copy(pooled_buf.at[0], pooled_ref.at[:, me], local_sem.at[2])
    own_pool.start()

    @pl.loop(0, GROUPS)
    def _(g):
        turn_cotangents(g)

    def grad_block(at):
        pieces = [counts[at * (SHARD // LOW) + j] for j in range(SHARD // LOW)]
        return jnp.dot(split[...], jnp.concatenate(pieces, 1), preferred_element_type=F32)

    def pair_copy(step):
        return remote(pair_out.at[step], pair_in.at[step], px_out.at[step], px_in.at[step], twin)

    def far_copy(n):
        return remote(far_out.at[n], far_in.at[n], far_sem_out.at[n], far_sem_in.at[n], ring(1 - 2 * n))

    def near_copy(n):
        return remote(near_out.at[n], near_in.at[n], near_sem_out.at[n], near_sem_in.at[n], ring(1 - 2 * n))

    def twin_block(step):
        pair_out[step] = grad_block(slot(step, 1)).astype(BF16)
        pair_copy(step).start()

    def own_block(step):
        own = grad_block(slot(step))
        pair_copy(step).wait_recv()
        return own + pair_in[step].astype(F32)

    twin_block(2)
    twin_block(1)
    total = own_block(2)
    for n in range(2):
        far_out[n] = total[n * 128 : (n + 1) * 128].astype(BF16)
        far_copy(n).start()
    twin_block(3)
    twin_block(0)
    pool_groups(EARLY, MIDDLE)
    for n in range(2):
        total = own_block(1 + 2 * n)
        far_copy(n).wait_recv()
        mine = slice(n * 128, (n + 1) * 128)
        rest = slice((1 - n) * 128, (2 - n) * 128)
        near_out[n, mine] = (total[mine] + far_in[n].astype(F32)).astype(BF16)
        near_out[n, rest] = total[rest].astype(BF16)
        near_copy(n).start()
    grad = own_block(0)
    pool_groups(MIDDLE, LATE)
    for n in range(2):
        near_copy(n).wait_recv()
        grad = grad + near_in[n].astype(F32)
    for t in range(2):
        one_grad = grad[t * 128 : (t + 1) * 128]
        sums = accum_ref[t : t + 1, :] + jnp.mean(one_grad * one_grad, axis=0, keepdims=True)
        new_sums[t : t + 1, :] = sums
        new_shard[t, rep] = table_ref[t] - (0.1 * one_grad / jnp.sqrt(sums)).T

    here = pl.ds(pl.multiple_of(rep * SHARD, SHARD), SHARD)
    own_sums = pltpu.make_async_copy(new_sums, new_accum_ref.at[:, here], local_sem.at[4])

    def sums_copy(r, at):
        where = pl.ds(pl.multiple_of(at * SHARD, SHARD), SHARD)
        return remote(new_sums, new_accum_ref.at[:, where], acc_out.at[r], acc_in.at[r], {"rep": (rep + r) % 8})

    spread = (new_out, new_in, new_twin_out, new_twin_in)
    spread_own(new_shard, *spread)

    for r in range(1, 8):
        sums_copy(r, rep).start()

    own_sums.start()
    pool_groups(LATE, GROUPS)
    spread_near(new_shard, *spread)
    spread_rest(new_shard, *spread)
    spread_end(new_shard, new_twin_out, new_twin_in)
    own_new = pltpu.make_async_copy(new_shard, new_table_ref, local_sem.at[3])
    own_new.start()

    @pl.loop(1, 8)
    def _(r):
        sums_copy(r, (rep - r + 8) % 8).wait_recv()

    for i in range(1, PEERS):
        pool_arrival(order(i)).wait_recv()

    own_pool.wait()
    own_new.wait()
    own_sums.wait()

    for k in range(1, PEERS):
        ids_copy(k).wait_send()
        cot_copy(k).wait_send()
        pool_copy(k).wait_send()

    spread_sent(shards, tab_out, tab_in, tab_twin_out, tab_twin_in)
    spread_sent(new_shard, *spread)
    for n in range(2):
        far_copy(n).wait_send()
        near_copy(n).wait_send()
    for step in range(4):
        pair_copy(step).wait_send()

    @pl.loop(1, 8)
    def _(r):
        sums_copy(r, rep).wait_send()


def local(table, accum, bag_rows, pooled_grad):
    samples, tables, pool_len = bag_rows.shape
    pairs = tables // 2
    ids = bag_rows.transpose(1, 2, 0).reshape(pairs, 2 * pool_len, samples)
    cot = pooled_grad.reshape(samples, pairs, 2, 128)
    rows = PEERS * CHUNK
    dma = pltpu.SemaphoreType.DMA
    pooled, new_table, new_accum = pl.pallas_call(
        step_kernel,
        out_shape=[
            jax.ShapeDtypeStruct((samples, pairs, 2, 128), BF16),
            jax.ShapeDtypeStruct((2, 8, SHARD, 128), F32),
            jax.ShapeDtypeStruct((2, 8 * SHARD), F32),
        ],
        in_specs=[
            pl.BlockSpec(memory_space=pltpu.VMEM),
            pl.BlockSpec(memory_space=pl.ANY),
            pl.BlockSpec(memory_space=pltpu.VMEM),
            pl.BlockSpec(memory_space=pltpu.VMEM),
        ],
        out_specs=[pl.BlockSpec(memory_space=pl.ANY)] * 3,
        scratch_shapes=[
            pltpu.VMEM((PEERS, 32, 128), jnp.int16),
            pltpu.VMEM((PEERS, 32, 128), jnp.int16),
            pltpu.VMEM((PEERS, CHUNK // 2, 2, 128), BF16),
            pltpu.VMEM((PEERS, CHUNK // 2, 2, 128), BF16),
            pltpu.VMEM((2, 8, SHARD, 128), BF16),
            pltpu.VMEM((HIGH * LOW, 256), BF16),
            pltpu.VMEM((32, 256), F32),
            pltpu.VMEM((32, 256), F32),
            pltpu.VMEM((HIGH, rows, LOW), BF16),
            pltpu.VMEM((256, rows), BF16),
            pltpu.VMEM((4, 256, SHARD), BF16),
            pltpu.VMEM((4, 256, SHARD), BF16),
            pltpu.VMEM((2, 128, SHARD), BF16),
            pltpu.VMEM((2, 128, SHARD), BF16),
            pltpu.VMEM((2, 256, SHARD), BF16),
            pltpu.VMEM((2, 256, SHARD), BF16),
            pltpu.VMEM((2, 8, SHARD, 128), F32),
            pltpu.VMEM((2, SHARD), F32),
        ]
        + [dma((PEERS,))] * 6
        + [dma((5,))]
        + [dma((8,))] * 4
        + [dma((4,))] * 6
        + [dma((8,))] * 6,
        compiler_params=pltpu.CompilerParams(collective_id=1, has_side_effects=True, vmem_limit_bytes=58 << 20),
        name="embedding_step",
    )(ids, cot, table, accum)
    return (pooled.reshape(samples, tables, 128), new_table.reshape(2, 8 * SHARD, 128), new_accum)


def solution(mesh):
    in_specs = (
        P("mod", "rep", None),
        P("mod", "rep"),
        P(("rep", "mod"), None, None),
        P(("rep", "mod"), None, None),
    )
    out_specs = (P(("rep", "mod"), None, None), P("mod", None, None), P("mod", None))
    return jax.shard_map(local, mesh=mesh, in_specs=in_specs, out_specs=out_specs, check_vma=False)
```

```python
import functools

import jax
import jax.numpy as jnp
from jax import lax
from jax.experimental import pallas as pl
from jax.experimental.pallas import tpu as pltpu
from jax.sharding import PartitionSpec as P

BF16, F32, I32 = jnp.bfloat16, jnp.float32, jnp.int32
SUB = 8
HIGH = 16
LOW = 128
SHARD = 256
PEERS = 32
CHUNK = 256
BATCHED = 4
GROUPS = PEERS // BATCHED
EARLY, MIDDLE, LATE = 6, 8, 8
STRIDE = 11
MESH = pl.DeviceIdType.MESH


def away(me, step, sign):
    x, y, z = me // 8, (me // 2) % 4, me % 2
    dx, dy, dz = step // 8, (step // 2) % 4, step % 2
    return ((x + sign * dx + 4) % 4) * 8 + ((y + sign * dy + 4) % 4) * 2 + (z + dz) % 2


def order(i):
    return (i * STRIDE) % PEERS


def step_kernel(
    wide_ids_ref, cot_ref, table_ref, accum_ref, pooled_ref, new_table_ref, new_accum_ref,
    ids_ref, ids_buf, cot_buf, pooled_buf, shards, both, high_key, low_key, counts, split,
    pair_out, pair_in, far_out, far_in, near_out, near_in, new_shard, new_sums,
    ids_out, ids_in, cot_out, cot_in, pool_out, pool_in, local_sem,
    tab_out, tab_in, tab_twin_out, tab_twin_in, px_out, px_in, far_sem_out, far_sem_in, near_sem_out, near_sem_in,
    new_out, new_in, new_twin_out, new_twin_in, acc_out, acc_in,
):
    me = lax.axis_index("mod")
    rep = lax.axis_index("rep")
    high, core = rep // 2, rep % 2
    twin = {"rep": high * 2 + 1 - core}

    x, y, z = me // 8, (me // 2) % 4, me % 2
    xs = [((x + d) % 4) * 8 for d in range(4)]
    ys = [((y + d) % 4) * 2 for d in range(4)]
    zs = [(z + d) % 2 for d in range(2)]

    def peer(k, sign):
        if not isinstance(k, int):
            return away(me, k, sign)
        return xs[(sign * (k // 8)) % 4] + ys[(sign * (k // 2)) % 4] + zs[k % 2]

    def ring(step):
        return {"rep": ((high + step + 4) % 4) * 2 + core}

    def remote(src, dst, out_sem, in_sem, device):
        return pltpu.make_async_remote_copy(
            src_ref=src, dst_ref=dst, send_sem=out_sem, recv_sem=in_sem, device_id=device, device_id_type=MESH
        )

    def ids_copy(k):
        return remote(ids_ref.at[peer(k, 1)], ids_buf.at[k], ids_out.at[k], ids_in.at[k], {"mod": peer(k, 1)})

    def cot_copy(k):
        return remote(cot_ref.at[:, peer(k, 1)], cot_buf.at[k], cot_out.at[k], cot_in.at[k], {"mod": peer(k, 1)})

    def pool_copy(k):
        return remote(pooled_buf.at[k], pooled_ref.at[:, me], pool_out.at[k], pool_in.at[k], {"mod": peer(k, -1)})

    def pool_arrival(k):
        return remote(
            pooled_buf.at[k], pooled_ref.at[:, peer(k, 1)], pool_out.at[k], pool_in.at[k], {"mod": peer(k, -1)}
        )

    def slot(offset, other=0):
        return ((high + offset + 4) % 4) * 2 + (core + other - 2 * core * other)

    def ring_near(ref, n, out_sem, in_sem, arrival=False):
        table, side = (n, 1) if n < 2 else (3 - n, -1)
        at = ref.at[table, slot(-side if arrival else 0)]
        return remote(at, at, out_sem.at[n], in_sem.at[n], ring(side))

    def ring_far(ref, n, out_sem, in_sem, arrival=False):
        table, side = (0, 1) if n == 0 else (1, -1)
        at = ref.at[table, slot(2 if arrival else -side)]
        return remote(at, at, out_sem.at[4 + n], in_sem.at[4 + n], ring(side))

    def twin_copy(ref, offset, table, out_sem, in_sem, arrival=False):
        at = ref.at[table, slot(offset, 1 if arrival else 0)]
        n = (offset + 4) % 4 * 2 + table
        return remote(at, at, out_sem.at[n], in_sem.at[n], twin)

    def spread_own(ref, out_sem, in_sem, twin_out, twin_in):
        for n in (0, 2, 1, 3):
            ring_near(ref, n, out_sem, in_sem).start()
        for table in range(2):
            twin_copy(ref, 0, table, twin_out, twin_in).start()

    def spread_near(ref, out_sem, in_sem, twin_out, twin_in):
        for n in range(2):
            ring_near(ref, 2 * n, out_sem, in_sem, True).wait_recv()
            ring_far(ref, n, out_sem, in_sem).start()
            twin_copy(ref, -1 if n == 0 else 1, n, twin_out, twin_in).start()

    def spread_rest(ref, out_sem, in_sem, twin_out, twin_in):
        for n in range(2):
            ring_near(ref, 2 * n + 1, out_sem, in_sem, True).wait_recv()
            twin_copy(ref, -1 if n == 0 else 1, 1 - n, twin_out, twin_in).start()
        for n in range(2):
            ring_far(ref, n, out_sem, in_sem, True).wait_recv()
            twin_copy(ref, 2, n, twin_out, twin_in).start()

    def spread_end(ref, twin_out, twin_in):
        for offset in range(4):
            for table in range(2):
                twin_copy(ref, offset, table, twin_out, twin_in, True).wait_recv()

    def spread_sent(ref, out_sem, in_sem, twin_out, twin_in):
        for n in range(4):
            ring_near(ref, n, out_sem, in_sem).wait_send()
        for n in range(2):
            ring_far(ref, n, out_sem, in_sem).wait_send()
        for offset in range(4):
            for table in range(2):
                twin_copy(ref, offset, table, twin_out, twin_in).wait_send()

    barrier = pltpu.get_barrier_semaphore()

    for k in range(1, PEERS):
        pl.semaphore_signal(barrier, inc=1, device_id={"mod": peer(k, 1)}, device_id_type=MESH)
    for r in range(1, 8):
        pl.semaphore_signal(barrier, inc=1, device_id={"rep": (rep + r) % 8}, device_id_type=MESH)

    own_cot = pltpu.make_async_copy(cot_ref.at[:, me], cot_buf.at[0], local_sem.at[1])
    own_cot.start()

    @pl.loop(0, PEERS)
    def _(k):
        ids_ref[k] = wide_ids_ref[k].astype(jnp.int16)

    ids_buf[0] = ids_ref[me]
    shards[0, rep] = table_ref[0].astype(BF16)
    shards[1, rep] = table_ref[1].astype(BF16)
    pl.semaphore_wait(barrier, PEERS - 1 + 7)

    for i in range(1, PEERS):
        ids_copy(order(i)).start()

    spread_own(shards, tab_out, tab_in, tab_twin_out, tab_twin_in)

    for i in range(1, PEERS):
        cot_copy(order(i)).start()

    own_cot.wait()

    lane = lax.broadcasted_iota(I32, (16, 256), 1)
    iota = lax.broadcasted_iota(I32, (16, 256), 0).astype(F32)
    one, zero = jnp.ones((16, 256), BF16), jnp.zeros((16, 256), BF16)
    sample3 = lax.broadcasted_iota(I32, (16, SUB, 128), 1)
    lane3 = lax.broadcasted_iota(I32, (16, SUB, 128), 2) // 32

    def count_chunks(first):
        for c in range(2):
            i = first + c
            k = order(i)

            if c > 0:
                ids_copy(k).wait_recv()
            else:

                @pl.when(i > 0)
                def _(k=k):
                    ids_copy(k).wait_recv()

        for c in range(2):
            ids = ids_buf[order(first + c)].astype(I32).astype(F32)
            turned = jnp.concatenate([ids] * 4, 0).T.reshape(16, SUB, 128)
            upper = jnp.sum(jnp.where(sample3 == lane3, turned, 0.0), axis=1)
            lower = jnp.sum(jnp.where(sample3 == lane3 + 4, turned, 0.0), axis=1)
            flat = jnp.concatenate([upper, lower], 1).astype(I32)
            high_key[c * 16 : (c + 1) * 16] = ((flat // LOW) * 16 + lane // 16).astype(F32)
            low_key[c * 16 : (c + 1) * 16] = (flat % LOW).astype(F32)
        base = pl.multiple_of(first * CHUNK, 2 * CHUNK)
        for b in range(32):
            high_row = jnp.broadcast_to(high_key[b : b + 1, :], (16, 256)).astype(BF16)
            low_row = jnp.broadcast_to(low_key[b : b + 1, :], (16, 256)).astype(BF16)
            high_hot = jnp.concatenate(
                [jnp.where(high_row == (iota + 16 * j).astype(BF16), one, zero) for j in range(HIGH)], 0
            )
            low_hot = jnp.concatenate(
                [jnp.where(low_row == (iota + 16 * j).astype(BF16), one, zero) for j in range(LOW // 16)], 0
            )
            out = lax.dot_general(high_hot, low_hot, (((1,), (1,)), ((), ())), preferred_element_type=F32).astype(BF16)
            for j in range(HIGH):
                counts[j, pl.ds(base + b * 16, 16), :] = out[j * 16 : (j + 1) * 16]

    parity = lax.broadcasted_iota(I32, (BATCHED * CHUNK, 128), 0) % 2
    odd = (lax.broadcasted_iota(I32, (128, CHUNK), 1) % 2).astype(F32).astype(BF16)

    def pool_group(g):
        base = pl.multiple_of(g * BATCHED * CHUNK, BATCHED * CHUNK)
        rows = jnp.concatenate([counts[j, pl.ds(base, BATCHED * CHUNK), :] for j in range(HIGH)], 1)
        sums = jnp.dot(rows, both[...], preferred_element_type=F32)
        picked = jnp.where(parity == 0, sums[:, :128], sums[:, 128:]).astype(BF16)
        for b in range(BATCHED):
            pooled_buf[order(g * BATCHED + b)] = picked[b * CHUNK : (b + 1) * CHUNK].reshape(CHUNK // 2, 2, 128)
        for b in range(BATCHED):
            i = g * BATCHED + b

            @pl.when(i > 0)
            def _(i=i):
                pool_copy(order(i)).start()

    def pool_groups(start, end):
        if end > start:

            @pl.loop(start, end)
            def _(g):
                pool_group(g)

    def turn_cotangents(g):
        @pl.loop(0, BATCHED)
        def _(b):
            i = g * BATCHED + b
            k = order(i)

            @pl.when(i > 0)
            def _():
                cot_copy(k).wait_recv()

            turned = cot_buf[k].reshape(CHUNK, 128).T
            at = pl.ds(pl.multiple_of(i * CHUNK, CHUNK), CHUNK)
            second = turned * odd
            split[0:128, at] = turned - second
            split[128:256, at] = second

    @pl.loop(0, GROUPS)
    def _(g):
        @pl.loop(0, BATCHED // 2)
        def _(b):
            count_chunks(g * BATCHED + 2 * b)

        @pl.when(g == 3)
        def _():
            spread_near(shards, tab_out, tab_in, tab_twin_out, tab_twin_in)

        @pl.when(g == 6)
        def _():
            spread_rest(shards, tab_out, tab_in, tab_twin_out, tab_twin_in)

    spread_end(shards, tab_twin_out, tab_twin_in)
    for j in range(8):
        both[j * SHARD : (j + 1) * SHARD, :] = jnp.concatenate([shards[0, j], shards[1, j]], 1)

    @pl.loop(0, EARLY)
    def _(g):
        pool_group(g)

    own_pool = pltpu.make_async_copy(pooled_buf.at[0], pooled_ref.at[:, me], local_sem.at[2])
    own_pool.start()

    @pl.loop(0, GROUPS)
    def _(g):
        turn_cotangents(g)

    def grad_block(at):
        pieces = [counts[at * (SHARD // LOW) + j] for j in range(SHARD // LOW)]
        return jnp.dot(split[...], jnp.concatenate(pieces, 1), preferred_element_type=F32)

    def pair_copy(step):
        return remote(pair_out.at[step], pair_in.at[step], px_out.at[step], px_in.at[step], twin)

    def far_copy(n):
        return remote(far_out.at[n], far_in.at[n], far_sem_out.at[n], far_sem_in.at[n], ring(1 - 2 * n))

    def near_copy(n):
        return remote(near_out.at[n], near_in.at[n], near_sem_out.at[n], near_sem_in.at[n], ring(1 - 2 * n))

    def twin_block(step):
        pair_out[step] = grad_block(slot(step, 1)).astype(BF16)
        pair_copy(step).start()

    def own_block(step):
        own = grad_block(slot(step))
        pair_copy(step).wait_recv()
        return own + pair_in[step].astype(F32)

    twin_block(2)
    twin_block(1)
    total = own_block(2)
    for n in range(2):
        far_out[n] = total[n * 128 : (n + 1) * 128].astype(BF16)
        far_copy(n).start()
    twin_block(3)
    twin_block(0)
    pool_groups(EARLY, MIDDLE)
    for n in range(2):
        total = own_block(1 + 2 * n)
        far_copy(n).wait_recv()
        mine = slice(n * 128, (n + 1) * 128)
        rest = slice((1 - n) * 128, (2 - n) * 128)
        near_out[n, mine] = (total[mine] + far_in[n].astype(F32)).astype(BF16)
        near_out[n, rest] = total[rest].astype(BF16)
        near_copy(n).start()
    grad = own_block(0)
    pool_groups(MIDDLE, LATE)
    for n in range(2):
        near_copy(n).wait_recv()
        grad = grad + near_in[n].astype(F32)
    for t in range(2):
        one_grad = grad[t * 128 : (t + 1) * 128]
        sums = accum_ref[t : t + 1, :] + jnp.mean(one_grad * one_grad, axis=0, keepdims=True)
        new_sums[t : t + 1, :] = sums
        new_shard[t, rep] = table_ref[t] - (0.1 * one_grad / jnp.sqrt(sums)).T

    here = pl.ds(pl.multiple_of(rep * SHARD, SHARD), SHARD)
    own_sums = pltpu.make_async_copy(new_sums, new_accum_ref.at[:, here], local_sem.at[4])

    def sums_copy(r, at):
        where = pl.ds(pl.multiple_of(at * SHARD, SHARD), SHARD)
        return remote(new_sums, new_accum_ref.at[:, where], acc_out.at[r], acc_in.at[r], {"rep": (rep + r) % 8})

    spread = (new_out, new_in, new_twin_out, new_twin_in)
    spread_own(new_shard, *spread)

    for r in range(1, 8):
        sums_copy(r, rep).start()

    own_sums.start()
    pool_groups(LATE, GROUPS)
    for k in range(1, PEERS):
        ids_copy(k).wait_send()
        cot_copy(k).wait_send()
    spread_near(new_shard, *spread)
    spread_rest(new_shard, *spread)
    for i in range(1, PEERS):
        pool_arrival(order(i)).wait_recv()
    spread_end(new_shard, new_twin_out, new_twin_in)
    own_new = pltpu.make_async_copy(new_shard, new_table_ref, local_sem.at[3])
    own_new.start()

    @pl.loop(1, 8)
    def _(r):
        sums_copy(r, (rep - r + 8) % 8).wait_recv()


    own_pool.wait()
    own_new.wait()
    own_sums.wait()

    for k in range(1, PEERS):
        pool_copy(k).wait_send()

    spread_sent(shards, tab_out, tab_in, tab_twin_out, tab_twin_in)
    spread_sent(new_shard, *spread)
    for n in range(2):
        far_copy(n).wait_send()
        near_copy(n).wait_send()
    for step in range(4):
        pair_copy(step).wait_send()

    @pl.loop(1, 8)
    def _(r):
        sums_copy(r, rep).wait_send()


def local(table, accum, bag_rows, pooled_grad):
    samples, tables, pool_len = bag_rows.shape
    pairs = tables // 2
    ids = bag_rows.transpose(1, 2, 0).reshape(pairs, 2 * pool_len, samples)
    cot = pooled_grad.reshape(samples, pairs, 2, 128)
    rows = PEERS * CHUNK
    dma = pltpu.SemaphoreType.DMA
    pooled, new_table, new_accum = pl.pallas_call(
        step_kernel,
        out_shape=[
            jax.ShapeDtypeStruct((samples, pairs, 2, 128), BF16),
            jax.ShapeDtypeStruct((2, 8, SHARD, 128), F32),
            jax.ShapeDtypeStruct((2, 8 * SHARD), F32),
        ],
        in_specs=[
            pl.BlockSpec(memory_space=pltpu.VMEM),
            pl.BlockSpec(memory_space=pl.ANY),
            pl.BlockSpec(memory_space=pltpu.VMEM),
            pl.BlockSpec(memory_space=pltpu.VMEM),
        ],
        out_specs=[pl.BlockSpec(memory_space=pl.ANY)] * 3,
        scratch_shapes=[
            pltpu.VMEM((PEERS, 32, 128), jnp.int16),
            pltpu.VMEM((PEERS, 32, 128), jnp.int16),
            pltpu.VMEM((PEERS, CHUNK // 2, 2, 128), BF16),
            pltpu.VMEM((PEERS, CHUNK // 2, 2, 128), BF16),
            pltpu.VMEM((2, 8, SHARD, 128), BF16),
            pltpu.VMEM((HIGH * LOW, 256), BF16),
            pltpu.VMEM((32, 256), F32),
            pltpu.VMEM((32, 256), F32),
            pltpu.VMEM((HIGH, rows, LOW), BF16),
            pltpu.VMEM((256, rows), BF16),
            pltpu.VMEM((4, 256, SHARD), BF16),
            pltpu.VMEM((4, 256, SHARD), BF16),
            pltpu.VMEM((2, 128, SHARD), BF16),
            pltpu.VMEM((2, 128, SHARD), BF16),
            pltpu.VMEM((2, 256, SHARD), BF16),
            pltpu.VMEM((2, 256, SHARD), BF16),
            pltpu.VMEM((2, 8, SHARD, 128), F32),
            pltpu.VMEM((2, SHARD), F32),
        ]
        + [dma((PEERS,))] * 6
        + [dma((5,))]
        + [dma((8,))] * 4
        + [dma((4,))] * 6
        + [dma((8,))] * 6,
        compiler_params=pltpu.CompilerParams(collective_id=1, has_side_effects=True, vmem_limit_bytes=58 << 20),
        name="embedding_step",
    )(ids, cot, table, accum)
    return (pooled.reshape(samples, tables, 128), new_table.reshape(2, 8 * SHARD, 128), new_accum)


def solution(mesh):
    in_specs = (
        P("mod", "rep", None),
        P("mod", "rep"),
        P(("rep", "mod"), None, None),
        P(("rep", "mod"), None, None),
    )
    out_specs = (P(("rep", "mod"), None, None), P("mod", None, None), P("mod", None))
    return jax.shard_map(local, mesh=mesh, in_specs=in_specs, out_specs=out_specs, check_vma=False)
```
